32 devices in a mesh: groups: 2 (over y), row: 16 (over z, x, core).
Axes of the slice: x: 2, y: 2, z: 4, core: 2. Of those that a mesh axis runs over, the one named last changes fastest.
Arguments:
- strain_data: float32 [32, 32, 24576], P('row', None, 'groups'), parts along dimension 2, may hold values from -6 to 6
Outputs:
- coherence: float32 [2, 24576, 12288], P(None, ('groups', 'row')), parts along dimension 1
The draws below stay inside these ranges and needn't reach their ends.
There are 2 independent parts, one for each index of `groups`. The reference program is written for one: setup_inputs(seed, part) draws one part's arguments, and reference() takes and returns one part's arrays. A program takes and returns all parts, laid end to end along the dimension named above; each array names one. Nothing has to cross between parts.
All inputs are finite; a program needn't handle non-finite values.
Results may differ from the reference program's by a relative error of at most 0.00008.
Values sent between devices are 32-bit elements; how exact they have to be, the bound alone decides.
A program may use at most 256 MiB of HBM per device.

```python
import jax
import jax.numpy as jnp
from jax import lax

CHANNELS = 12288
SAMPLES = 32
FBIN = 5
PANES = 32


def block_levels(stream_key, dims, pieces, smallest, largest):
    loudness = 1.0
    for axis_at, blocks in pieces:
        heights = jax.random.uniform(jax.random.fold_in(jax.random.fold_in(stream_key, 6), axis_at), (blocks,), jnp.float32, smallest / len(pieces), largest / len(pieces))
        loudness = loudness * jnp.repeat(jnp.exp(heights), dims[axis_at] // blocks).reshape((-1,) + (1,) * (len(dims) - 1 - axis_at))
    return loudness


def gaussian(rng, extent, width, reach, cuts=(), held_as=jnp.bfloat16):
    entries = jax.random.normal(rng, extent, jnp.float32) * width
    if len(cuts) > 0:
        entries = block_levels(rng, extent, cuts, -0.22, 0.18) * entries
    return jnp.clip(entries, min=-reach, max=reach).astype(held_as)


def setup_inputs(seed: int = 0, part: int = 0) -> dict:
    key_list = jax.random.split(jax.random.key(seed), 2)
    own_keys = jax.random.split(jax.random.fold_in(key_list[1], part), 2)
    strain_data = gaussian(own_keys[0], (PANES, SAMPLES, CHANNELS), 1.0, 6.0, ((0, 16),), jnp.float32)
    return {"strain_data": strain_data}


def project(strain_data):
    samples = strain_data.shape[1]
    position = jnp.arange(samples, dtype=jnp.float32)
    taper = 0.5 - 0.5 * jnp.cos(2.0 * jnp.pi * (position + 0.5) / samples)
    phase = 2.0 * jnp.pi * FBIN * position / samples
    weights = jnp.stack([taper * jnp.cos(phase), -taper * jnp.sin(phase)])
    rms = jnp.sqrt(lax.optimization_barrier(jnp.mean(strain_data * strain_data, axis=1, keepdims=True)))
    normed = strain_data / jnp.maximum(rms, 1.0)
    return jnp.einsum('ks,psc->kpc', weights, normed, precision=lax.Precision.HIGHEST)

def cross(left, right):
    real_part = jnp.einsum('pa,pb->ab', left[0], right[0], precision=lax.Precision.HIGHEST) + jnp.einsum('pa,pb->ab', left[1], right[1], precision=lax.Precision.HIGHEST)
    imag_part = jnp.einsum('pa,pb->ab', left[1], right[0], precision=lax.Precision.HIGHEST) - jnp.einsum('pa,pb->ab', left[0], right[1], precision=lax.Precision.HIGHEST)
    return jnp.stack([real_part, imag_part])

def reference(strain_data):
    spectrum = project(strain_data)
    power = lax.optimization_barrier(jnp.sum(spectrum * spectrum, axis=(0, 1)))
    scale = lax.rsqrt(power + 1e-06)
    return cross(spectrum, spectrum) * scale[None, :, None] * scale[None, None, :]
```

```python
import jax
import jax.numpy as jnp
import numpy as np
from jax import lax
from jax.experimental import pallas as pl
from jax.experimental.pallas import tpu as pltpu
from jax.sharding import PartitionSpec as P

FBIN = 5


def divisor(size, largest):
    return max(w for w in range(128, largest + 1, 128) if size % w == 0)


def taper_weights(samples):
    position = np.arange(samples)
    taper = 0.5 - 0.5 * np.cos(2.0 * np.pi * (position + 0.5) / samples)
    phase = 2.0 * np.pi * FBIN * position / samples
    return np.stack([taper * np.cos(phase), -taper * np.sin(phase)]).astype(np.float32)


def project_kernel(weights_ref, strain_ref, out_ref):
    panes, samples, _ = strain_ref.shape
    for p in range(panes):
        x = strain_ref[p]
        rms = jnp.sqrt(jnp.sum(x * x, axis=0, keepdims=True) * (1.0 / samples))
        inverse = 1.0 / jnp.maximum(rms, 1.0)
        for k in range(2):
            total = jnp.sum(x * weights_ref[k], axis=0, keepdims=True) * inverse
            out_ref[0, pl.ds(k * panes + p, 1), :] = total


def project(strain):
    panes, samples, channels = strain.shape
    width = divisor(channels, 2048)
    weights = jnp.asarray(taper_weights(samples))[:, :, None]
    return pl.pallas_call(
        project_kernel,
        grid=(channels // width,),
        in_specs=[
            pl.BlockSpec((2, samples, 1), lambda j: (0, 0, 0)),
            pl.BlockSpec((panes, samples, width), lambda j: (0, 0, j)),
        ],
        out_specs=pl.BlockSpec((1, 2 * panes, width), lambda j: (0, 0, j)),
        out_shape=jax.ShapeDtypeStruct((1, 2 * panes, channels), jnp.float32),
    )(weights, strain)


def scaled(g):
    power = jnp.sum(g * g, axis=0, keepdims=True)
    return g * lax.rsqrt(power + 1e-06)


def halves(x):
    high = x.astype(jnp.bfloat16)
    return high, (x - high.astype(jnp.float32)).astype(jnp.bfloat16)


def cross_kernel(own_ref, all_ref, out_ref, left_ref):
    devices, rows, block = all_ref.shape
    depth = devices * rows
    panes = rows // 2

    @pl.when(pl.program_id(0) == 0)
    def _():
        own = scaled(own_ref[...].reshape(depth, own_ref.shape[2]))
        split = own.reshape(devices, rows, own.shape[1])
        turned = jnp.concatenate([split[:, panes:], -split[:, :panes]], axis=1)
        for part, u in enumerate((own, turned.reshape(own.shape))):
            high, low = halves(u.T)
            left_ref[part] = jnp.concatenate([high, low, high], axis=1)

    high, low = halves(scaled(all_ref[...].reshape(depth, block)))
    right = jnp.concatenate([high, high, low], axis=0)
    for part in range(2):
        out_ref[part] = jnp.dot(
            left_ref[part], right, preferred_element_type=jnp.float32
        )


def cross(own, gathered):
    devices, rows, channels = gathered.shape
    width = own.shape[2]
    block = divisor(channels, 512)
    depth = 3 * devices * rows
    return pl.pallas_call(
        cross_kernel,
        grid=(channels // block,),
        in_specs=[
            pl.BlockSpec((devices, rows, width), lambda j: (0, 0, 0)),
            pl.BlockSpec((devices, rows, block), lambda j: (0, 0, j)),
        ],
        out_specs=pl.BlockSpec((2, width, block), lambda j: (0, 0, j)),
        out_shape=jax.ShapeDtypeStruct((2, width, channels), jnp.float32),
        scratch_shapes=[pltpu.VMEM((2, width, depth), jnp.bfloat16)],
        compiler_params=pltpu.CompilerParams(vmem_limit_bytes=48 * 1024 * 1024),
    )(own, gathered)


def on_device(strain_data):
    channels = strain_data.shape[2]
    width = channels // lax.axis_size("row")
    offset = lax.axis_index("row") * width
    gathered = lax.all_gather(project(strain_data), "row", axis=0, tiled=True)
    own = lax.dynamic_slice_in_dim(gathered, offset, width, 2)
    return cross(own, gathered)


def solution(mesh):
    in_specs = (P("row", None, "groups"),)
    out_specs = P(None, ("groups", "row"), None)
    return jax.shard_map(
        on_device, mesh=mesh, in_specs=in_specs, out_specs=out_specs, check_vma=False
    )
```

```python
import functools

import jax
import jax.numpy as jnp
import numpy as np
from jax import lax
from jax.experimental import pallas as pl
from jax.experimental.pallas import tpu as pltpu
from jax.sharding import PartitionSpec as P

FBIN = 5


def divisor(size, largest):
    return max(w for w in range(128, largest + 1, 128) if size % w == 0)


def taper_weights(samples):
    position = np.arange(samples)
    taper = 0.5 - 0.5 * np.cos(2.0 * np.pi * (position + 0.5) / samples)
    phase = 2.0 * np.pi * FBIN * position / samples
    return np.stack([taper * np.cos(phase), -taper * np.sin(phase)]).astype(np.float32)


def project_kernel(weights_ref, strain_ref, out_ref):
    panes, samples, _ = strain_ref.shape
    for p in range(panes):
        x = strain_ref[p]
        rms = jnp.sqrt(jnp.sum(x * x, axis=0, keepdims=True) * (1.0 / samples))
        inverse = 1.0 / jnp.maximum(rms, 1.0)
        for k in range(2):
            total = jnp.sum(x * weights_ref[k], axis=0, keepdims=True) * inverse
            out_ref[0, pl.ds(k * panes + p, 1), :] = total


def project(strain):
    panes, samples, channels = strain.shape
    width = divisor(channels, 2048)
    weights = jnp.asarray(taper_weights(samples))[:, :, None]
    return pl.pallas_call(
        project_kernel,
        grid=(channels // width,),
        in_specs=[
            pl.BlockSpec((2, samples, 1), lambda j: (0, 0, 0)),
            pl.BlockSpec((panes, samples, width), lambda j: (0, 0, j)),
        ],
        out_specs=pl.BlockSpec((1, 2 * panes, width), lambda j: (0, 0, j)),
        out_shape=jax.ShapeDtypeStruct((1, 2 * panes, channels), jnp.float32),
    )(weights, strain)


def gather_kernel(devices, x_ref, out_ref, local_sem, ring_send, ring_recv, pair_send, pair_recv):
    chips, half = devices // 2, devices // 4
    columns = out_ref.shape[2] // 2
    me = lax.axis_index("row")
    core = me % 2
    chip = me // 2
    position = chip // 2 + (chip % 2) * (chips - 1 - 2 * (chip // 2))
    sibling = me + 1 - 2 * core

    def device_at(shift):
        p = (position + chips + shift) % chips
        back = p // half
        return 2 * (2 * p + back * (2 * (chips - 1 - p) + 1 - 2 * p)) + core

    def piece(ref, direction, last):
        return ref.at[:, pl.ds(direction * columns, columns)] if last else ref

    def ring_copy(direction, step):
        ahead = 1 - 2 * direction
        origin = device_at(-ahead * step)
        source = x_ref.at[0] if step == 0 else out_ref.at[origin]
        last = step == half - 1
        return pltpu.make_async_remote_copy(
            src_ref=piece(source, direction, last),
            dst_ref=piece(out_ref.at[origin], direction, last),
            send_sem=ring_send.at[2 * step + direction],
            recv_sem=ring_recv.at[2 * step + direction],
            device_id={"row": device_at(ahead)},
            device_id_type=pl.DeviceIdType.MESH,
        )

    def pair_copy(direction, step):
        ahead = 1 - 2 * direction
        origin = device_at(-ahead * step)
        block = piece(out_ref.at[origin], direction, step == half)
        source = x_ref.at[0] if step == 0 else block
        index = 2 * step + direction
        return pltpu.make_async_remote_copy(
            src_ref=source,
            dst_ref=block,
            send_sem=pair_send.at[index],
            recv_sem=pair_recv.at[index],
            device_id={"row": sibling},
            device_id_type=pl.DeviceIdType.MESH,
        )

    barrier = pltpu.get_barrier_semaphore()
    for partner in (device_at(1), device_at(-1), sibling):
        pl.semaphore_signal(
            barrier, inc=1, device_id={"row": partner}, device_id_type=pl.DeviceIdType.MESH
        )
    pl.semaphore_wait(barrier, 3)

    ring = {(d, 0): ring_copy(d, 0) for d in range(2)}
    for copy in ring.values():
        copy.start()
    own = pltpu.make_async_copy(x_ref.at[0], out_ref.at[me], local_sem)
    own.start()
    pairs = [pair_copy(0, 0)]
    pairs[0].start()
    for step in range(half):
        for d in range(2):
            ring[d, step].wait_recv()
            if step + 1 < half:
                ring[d, step + 1] = ring_copy(d, step + 1)
                ring[d, step + 1].start()
            pairs.append(pair_copy(d, step + 1))
            pairs[-1].start()
    own.wait()
    for copy in ring.values():
        copy.wait_send()
    for copy in pairs:
        copy.wait()


def gather(spectrum):
    devices = lax.axis_size("row")
    _, rows, channels = spectrum.shape
    copies = devices // 2
    return pl.pallas_call(
        functools.partial(gather_kernel, devices),
        in_specs=[pl.BlockSpec(memory_space=pl.ANY)],
        out_specs=pl.BlockSpec(memory_space=pl.ANY),
        out_shape=jax.ShapeDtypeStruct((devices, rows, channels), jnp.float32),
        scratch_shapes=[
            pltpu.SemaphoreType.DMA,
            pltpu.SemaphoreType.DMA((copies,)),
            pltpu.SemaphoreType.DMA((copies,)),
            pltpu.SemaphoreType.DMA((copies + 2,)),
            pltpu.SemaphoreType.DMA((copies + 2,)),
        ],
        compiler_params=pltpu.CompilerParams(collective_id=0, has_side_effects=True),
    )(spectrum)


def scaled(g):
    power = jnp.sum(g * g, axis=0, keepdims=True)
    return g * lax.rsqrt(power + 1e-06)


def halves(x):
    high = x.astype(jnp.bfloat16)
    return high, (x - high.astype(jnp.float32)).astype(jnp.bfloat16)


def cross_kernel(own_ref, all_ref, out_ref, left_ref):
    devices, rows, block = all_ref.shape
    depth = devices * rows
    panes = rows // 2

    @pl.when(pl.program_id(0) == 0)
    def _():
        own = scaled(own_ref[...].reshape(depth, own_ref.shape[2]))
        split = own.reshape(devices, rows, own.shape[1])
        turned = jnp.concatenate([split[:, panes:], -split[:, :panes]], axis=1)
        for part, u in enumerate((own, turned.reshape(own.shape))):
            high, low = halves(u.T)
            left_ref[part] = jnp.concatenate([high, low, high], axis=1)

    high, low = halves(scaled(all_ref[...].reshape(depth, block)))
    right = jnp.concatenate([high, high, low], axis=0)
    for part in range(2):
        out_ref[part] = jnp.dot(
            left_ref[part], right, preferred_element_type=jnp.float32
        )


def cross(own, gathered):
    devices, rows, channels = gathered.shape
    width = own.shape[2]
    block = divisor(channels, 512)
    depth = 3 * devices * rows
    return pl.pallas_call(
        cross_kernel,
        grid=(channels // block,),
        in_specs=[
            pl.BlockSpec((devices, rows, width), lambda j: (0, 0, 0)),
            pl.BlockSpec((devices, rows, block), lambda j: (0, 0, j)),
        ],
        out_specs=pl.BlockSpec((2, width, block), lambda j: (0, 0, j)),
        out_shape=jax.ShapeDtypeStruct((2, width, channels), jnp.float32),
        scratch_shapes=[pltpu.VMEM((2, width, depth), jnp.bfloat16)],
        compiler_params=pltpu.CompilerParams(vmem_limit_bytes=48 * 1024 * 1024),
    )(own, gathered)


def on_device(strain_data):
    channels = strain_data.shape[2]
    width = channels // lax.axis_size("row")
    offset = lax.axis_index("row") * width
    gathered = gather(project(strain_data))
    own = lax.dynamic_slice_in_dim(gathered, offset, width, 2)
    return cross(own, gathered)


def solution(mesh):
    in_specs = (P("row", None, "groups"),)
    out_specs = P(None, ("groups", "row"), None)
    return jax.shard_map(
        on_device, mesh=mesh, in_specs=in_specs, out_specs=out_specs, check_vma=False
    )
```
